32 devices in a mesh: date: 2 (over x), trade: 16 (over z, y, core).
Axes of the slice: x: 2, y: 2, z: 4, core: 2. Of those that a mesh axis runs over, the one named last changes fastest.
Arguments:
- initial_term_structure: float32 [48], replicated, may hold values from 0.01 to 0.06
- long_level: float32 [48], replicated, may hold values from 0.01 to 0.07
- reversion: float32 [48], replicated, may hold values from 0.02 to 2
- volatility: float32 [48], replicated, may hold values from 0.002 to 0.01
- mixing: float32 [48, 48], replicated, may hold values from -0.875 to 0.875
- shocks: float32 [4, 48, 512], P('date'), may hold values from -6 to 6
- cashflows: bfloat16 [48, 131072], P(None, 'trade'), may hold values from -0.01953125 to 0.01953125
- maturity: int32 [131072], P('trade'), may hold values from 1 to 4, as said below
- netting: int32 [131072], P('trade'), may hold values from 0 to 63
Outputs:
- exposure: float32 [4, 64], P('date', 'trade')
The draws below stay inside these ranges and needn't reach their ends.
Inputs may be any that keep to these rules, and one draw needn't show every extreme that they name: Trades are grouped by maturity along trade: the trades held by one device mature within a narrow band of dates that rises with the device's index.
All inputs are finite; a program needn't handle non-finite values.
Results may differ from the reference program's by a relative error of at most 0.003.
Values may be sent and summed in bfloat16 or wider, within the bound.
A program may use at most 64 MiB of HBM per device.

```python
import math
import jax
import jax.numpy as jnp
from jax import lax

FACTORS = 48
PATHS = 512
TR_DEV = 8192
SETS_DEV = 4
DATES = 4
CONTRACT_COUNT = 131072
SETS = 64


def draw_maturity(key, part):
    index = jnp.arange(CONTRACT_COUNT, dtype=jnp.int32)
    owner = index // TR_DEV
    holders = CONTRACT_COUNT // TR_DEV
    lower = 1 + owner * (DATES - 1) // holders
    upper = 1 + (owner + 1) * (DATES - 1) // holders
    raw = jax.random.randint(key, (CONTRACT_COUNT,), 0, 1 << 20, dtype=jnp.int32)
    picked = lower + raw % (upper - lower + 1)
    return jnp.where(index % TR_DEV == 0, upper, picked).astype(jnp.int32)


def touch_ends(result, stream_key, smallest, high):
    dims = result.shape
    place = [jax.random.randint(jax.random.fold_in(stream_key, axis), (), 0, dims[axis]) for axis in range(len(dims))]
    result = result.at[tuple(place)].set(smallest)
    longest = dims.index(max(dims))
    place[longest] = (place[longest] + 1) % dims[longest]
    return result.at[tuple(place)].set(high)


def shard_levels(rng, shape, split, smallest, high):
    factor_of = 1.0
    for position, blocks in split:
        draws = jax.random.uniform(jax.random.fold_in(jax.random.fold_in(rng, 6), position), (blocks,), jnp.float32, smallest / len(split), high / len(split))
        factor_of = factor_of * jnp.repeat(jnp.exp(draws), shape[position] // blocks).reshape((-1,) + (1,) * (len(shape) - 1 - position))
    return factor_of


def centred(stream_key, dims, scale, bound, pieces=(), kind=jnp.bfloat16):
    array = jax.random.normal(stream_key, dims, jnp.float32) * scale
    if len(pieces) > 0:
        array = shard_levels(stream_key, dims, pieces, -0.22, 0.18) * array
    return jnp.clip(array, min=-bound, max=bound).astype(kind)


def setup_inputs(seed: int = 0) -> dict:
    keys = jax.random.split(jax.random.key(seed), 10)
    initial_term_structure = jnp.clip(jax.random.uniform(keys[0], (FACTORS,), jnp.float32, 0.01, 0.06), 0.01, 0.06)
    long_level = jnp.clip(jax.random.uniform(keys[1], (FACTORS,), jnp.float32, 0.01, 0.07), 0.01, 0.07)
    reversion = jnp.clip(jnp.exp(jax.random.uniform(keys[2], (FACTORS,), jnp.float32, math.log(0.02), math.log(2.0))), 0.02, 2.0)
    volatility = jnp.clip(jnp.exp(jax.random.uniform(keys[3], (FACTORS,), jnp.float32, math.log(0.002), math.log(0.01))), 0.002, 0.01)
    mixing = centred(keys[4], (FACTORS, FACTORS), FACTORS ** -0.5, 0.875, (), jnp.float32)
    shocks = centred(keys[5], (DATES, FACTORS, PATHS), 1.0, 6.0, ((0, 2),), jnp.float32)
    cashflows = centred(keys[6], (FACTORS, CONTRACT_COUNT), (FACTORS * TR_DEV // SETS_DEV) ** -0.5, 0.01953125, ((1, 16),))
    maturity = draw_maturity(jax.random.fold_in(keys[9], 71), 0)
    netting = touch_ends(jax.random.randint(keys[8], (CONTRACT_COUNT,), 0, SETS), jax.random.fold_in(keys[8], 1), 0, SETS - 1).astype(jnp.int32)
    return {"initial_term_structure": initial_term_structure, "long_level": long_level, "reversion": reversion, "volatility": volatility, "mixing": mixing, "shocks": shocks, "cashflows": cashflows, "maturity": maturity, "netting": netting}


def reference(initial_term_structure, long_level, reversion, volatility, mixing, shocks, cashflows, maturity, netting):
    decay = jnp.exp(-0.25 * reversion)
    drift = (1.0 - decay) * long_level
    tenor = 0.25 * (jnp.arange(FACTORS, dtype=jnp.int32).astype(jnp.float32) + 1.0)
    y_start = jnp.broadcast_to(initial_term_structure[:, None], (FACTORS, PATHS)).astype(jnp.float32)

    def advance(y_prev, shock):
        moved = jnp.dot(mixing, shock, precision=lax.Precision.HIGHEST)
        y_next = decay[:, None] * y_prev + drift[:, None] + volatility[:, None] * moved
        return y_next, y_next

    _, yields = lax.scan(advance, y_start, shocks)
    dates = jnp.arange(DATES, dtype=jnp.int32)
    cash_rows = cashflows.astype(jnp.float32).T

    def per_date(item):
        y_now, valuation_date = item
        discount = jnp.exp(-y_now * tenor[:, None]).astype(jnp.bfloat16).astype(jnp.float32)
        weight = jnp.maximum(maturity - valuation_date, 0).astype(jnp.float32) / maturity.astype(jnp.float32)
        set_rows = jax.ops.segment_sum(cash_rows * weight[:, None], netting, SETS)
        value = jnp.dot(set_rows, discount, precision=lax.Precision.HIGHEST)
        return jnp.mean(jnp.maximum(value, 0.0), axis=1)

    return lax.map(per_date, (yields, dates))
```

```python
import functools

import jax
import jax.numpy as jnp
from jax import lax
from jax.experimental import pallas as pl
from jax.experimental.pallas import tpu as pltpu
from jax.sharding import PartitionSpec as P

SETS_DEV = 4
LANES = 128
MESH = pl.DeviceIdType.MESH


def each(count, body):
    if count <= 16:
        for index in range(count):
            body(index)
    else:
        pl.loop(0, count)(body)


def split(x):
    high = x.astype(jnp.bfloat16)
    low = (x - high.astype(jnp.float32)).astype(jnp.bfloat16)
    return high, low


def kernel(
    dates_dev,
    dates_n,
    trade_n,
    start_ref,
    level_ref,
    speed_ref,
    vol_ref,
    mixing_ref,
    shocks_hbm,
    cash_hbm,
    maturity_ref,
    netting_ref,
    out_ref,
    shocks_v,
    cash_v,
    code_v,
    acc_v,
    offset_v,
    state_v,
    leave_v,
    arrive_v,
    send_v,
    recv_v,
    shock_sem,
    cash_sem,
    leave_sem,
    arrive_sem,
    send_sem,
    recv_sem,
):
    factors, trades = cash_v.shape
    paths = shocks_v.shape[2]
    chunks = cash_sem.shape[0]
    chunk = trades // chunks
    sets_all = SETS_DEV * trade_n
    maturities = dates_dev * dates_n
    width = send_v.shape[2]
    date = lax.axis_index("date")
    me = lax.axis_index("trade")

    shock_copy = pltpu.make_async_copy(shocks_hbm, shocks_v, shock_sem)
    shock_copy.start()

    def cash_copy(index):
        part = pl.ds(pl.multiple_of(index * chunk, chunk), chunk)
        return pltpu.make_async_copy(cash_hbm.at[:, part], cash_v.at[:, part], cash_sem.at[index])

    for index in range(chunks):
        cash_copy(index).start()

    barrier = pltpu.get_barrier_semaphore()

    def greet(index):
        other = lax.rem(me + 1 + index, trade_n)
        pl.semaphore_signal(barrier, inc=1, device_id={"trade": other}, device_id_type=MESH)

    each(trade_n - 1, greet)

    @pl.when(date > 0)
    def _():
        pl.semaphore_signal(barrier, inc=1, device_id={"date": date - 1}, device_id_type=MESH)

    diagonal = lax.broadcasted_iota(jnp.int32, (factors, factors), 0) == lax.broadcasted_iota(
        jnp.int32, (factors, factors), 1
    )

    def column(ref):
        return jnp.sum(jnp.where(diagonal, ref[...], 0.0), axis=1, keepdims=True)

    decay = jnp.exp(-0.25 * column(speed_ref))
    drift = (1.0 - decay) * column(level_ref)
    start = jnp.broadcast_to(column(start_ref), (factors, paths))
    mix_high, mix_low = split(column(vol_ref) * mixing_ref[...])
    mix = jnp.concatenate([mix_high, mix_high, mix_low], axis=1)

    for m in range(1, maturities + 1):
        code_v[m - 1] = jnp.where(maturity_ref[...] == m, netting_ref[...], -1).astype(jnp.float32)

    shock_copy.wait()
    running = None
    power = jnp.ones_like(decay)
    for step in range(dates_dev):
        high, low = split(shocks_v[step])
        moved = jnp.dot(
            mix, jnp.concatenate([high, low, high], axis=0), preferred_element_type=jnp.float32
        )
        running = drift + moved if step == 0 else decay * running + drift + moved
        power = power * decay
        offset_v[step] = running

    leave_copy = pltpu.make_async_remote_copy(
        src_ref=leave_v,
        dst_ref=arrive_v,
        send_sem=leave_sem,
        recv_sem=arrive_sem,
        device_id={"date": date + 1},
        device_id_type=MESH,
    )

    def leave(state):
        leave_v[...] = (power * state + running).astype(jnp.bfloat16)
        leave_copy.start()

    pl.semaphore_wait(barrier, trade_n - 1 + (date < dates_n - 1).astype(jnp.int32))

    @pl.when(date == 0)
    def _():
        state_v[...] = start
        leave(start)

    if dates_n > 2:

        @pl.when(jnp.logical_and(date > 0, date < dates_n - 1))
        def _():
            leave_copy.wait_recv()
            state = arrive_v[...].astype(jnp.float32)
            state_v[...] = state
            leave(state)

    tiles = sets_all // 16
    place = lax.broadcasted_iota(jnp.int32, (16, LANES), 0).astype(jnp.float32)
    marks = [(place + 16.0 * i).astype(jnp.bfloat16) for i in range(tiles)]
    one = jnp.ones((16, LANES), jnp.bfloat16)
    zero = jnp.zeros((16, LANES), jnp.bfloat16)
    rows = chunk // LANES

    def members(m, index):
        pieces = []
        for r in range(rows):
            code = jnp.broadcast_to(code_v[m, pl.ds(index * rows + r, 1), :], (16, LANES))
            code = code.astype(jnp.bfloat16)
            pieces.append(
                jnp.concatenate([jnp.where(code == mark, one, zero) for mark in marks], axis=0)
            )
        return jnp.concatenate(pieces, axis=1)

    def summed(member, index):
        cash = cash_v[:, pl.ds(pl.multiple_of(index * chunk, chunk), chunk)]
        cash = jnp.concatenate([cash] * dates_dev, axis=0)
        return lax.dot_general(
            member, cash, (((1,), (1,)), ((), ())), preferred_element_type=jnp.float32
        )

    lane = lax.broadcasted_iota(jnp.int32, (1, dates_dev * factors), 1)
    at_date = date * dates_dev + lane // factors

    def weight(m):
        return jnp.maximum(m - at_date, 0).astype(jnp.float32) / jnp.full_like(
            at_date, m
        ).astype(jnp.float32)

    if maturities * sets_all <= 256:
        total = jnp.zeros((maturities * sets_all, dates_dev * factors), jnp.float32)
        for index in range(chunks):
            cash_copy(index).wait()
            member = jnp.concatenate([members(m, index) for m in range(maturities)], axis=0)
            total = total + summed(member, index)
        held = jnp.zeros((sets_all, dates_dev * factors), jnp.float32)
        for m in range(maturities):
            held = held + weight(m + 1) * total[m * sets_all : (m + 1) * sets_all]
    else:
        acc_v[...] = jnp.zeros_like(acc_v)
        for index in range(chunks):
            cash_copy(index).wait()

        @pl.loop(0, chunks)
        def _(index):
            @pl.loop(0, maturities)
            def _(m):
                acc_v[...] += weight(m + 1) * summed(members(m, index), index)

        held = acc_v[...]

    send_v[...] = jnp.zeros_like(send_v)
    for owner in range(trade_n):
        send_v[owner, :, : dates_dev * factors] = held[owner * SETS_DEV : (owner + 1) * SETS_DEV]

    def push(index):
        other = lax.rem(me + 1 + index, trade_n)
        pltpu.make_async_remote_copy(
            src_ref=send_v.at[other],
            dst_ref=recv_v.at[index],
            send_sem=send_sem,
            recv_sem=recv_sem,
            device_id={"trade": other},
            device_id_type=MESH,
        ).start()

    each(trade_n - 1, push)

    @pl.when(date == dates_n - 1)
    def _():
        leave_copy.wait_recv()
        state_v[...] = arrive_v[...].astype(jnp.float32)

    tenor = 0.25 * (
        lax.broadcasted_iota(jnp.int32, (factors, 1), 0).astype(jnp.float32) + 1.0
    )
    discounts = []
    power = jnp.ones_like(decay)
    for step in range(dates_dev):
        power = power * decay
        now = power * state_v[...] + offset_v[step]
        discounts.append(jnp.exp(-now * tenor).astype(jnp.bfloat16))
    if width > dates_dev * factors:
        discounts.append(jnp.zeros((width - dates_dev * factors, paths), jnp.bfloat16))
    discount = jnp.concatenate(discounts, axis=0)

    everything = pltpu.make_async_copy(recv_v, recv_v, recv_sem)
    everything.wait()
    owned = send_v[me] + jnp.sum(recv_v[...], axis=0)
    lane = lax.broadcasted_iota(jnp.int32, owned.shape, 1) // factors
    owned = jnp.concatenate([jnp.where(lane == step, owned, 0.0) for step in range(dates_dev)], axis=0)
    high, low = split(owned)
    value = jnp.dot(high, discount, preferred_element_type=jnp.float32) + jnp.dot(
        low, discount, preferred_element_type=jnp.float32
    )
    mean = jnp.sum(jnp.maximum(value, 0.0), axis=1, keepdims=True) / paths
    pick = lax.broadcasted_iota(jnp.int32, (SETS_DEV, SETS_DEV), 0) == lax.broadcasted_iota(
        jnp.int32, (SETS_DEV, SETS_DEV), 1
    )
    for step in range(dates_dev):
        part = mean[step * SETS_DEV : (step + 1) * SETS_DEV]
        out_ref[step : step + 1, :] = jnp.sum(jnp.where(pick, part, 0.0), axis=0, keepdims=True)

    pltpu.make_async_copy(recv_v, recv_v, send_sem).wait()

    @pl.when(date < dates_n - 1)
    def _():
        leave_copy.wait_send()


def per_device(
    initial_term_structure,
    long_level,
    reversion,
    volatility,
    mixing,
    shocks,
    cashflows,
    maturity,
    netting,
):
    dates_dev, factors, paths = shocks.shape
    trades = cashflows.shape[1]
    dates_n = lax.axis_size("date")
    trade_n = lax.axis_size("trade")
    sets_all = SETS_DEV * trade_n
    width = -(-dates_dev * factors // LANES) * LANES
    chunks = max(1, trades // 1024)
    row = lambda x: x.reshape(1, factors)
    tall = lambda x: x.reshape(trades // LANES, LANES)
    vmem = pl.BlockSpec(memory_space=pltpu.VMEM)
    hbm = pl.BlockSpec(memory_space=pl.ANY)
    return pl.pallas_call(
        functools.partial(kernel, dates_dev, dates_n, trade_n),
        out_shape=jax.ShapeDtypeStruct((dates_dev, SETS_DEV), jnp.float32),
        in_specs=[vmem] * 5 + [hbm] * 2 + [vmem] * 2,
        out_specs=vmem,
        scratch_shapes=[
            pltpu.VMEM((dates_dev, factors, paths), jnp.float32),
            pltpu.VMEM((factors, trades), jnp.bfloat16),
            pltpu.VMEM((dates_dev * dates_n, trades // LANES, LANES), jnp.float32),
            pltpu.VMEM((sets_all, dates_dev * factors), jnp.float32),
            pltpu.VMEM((dates_dev, factors, paths), jnp.float32),
            pltpu.VMEM((factors, paths), jnp.float32),
            pltpu.VMEM((factors, paths), jnp.bfloat16),
            pltpu.VMEM((factors, paths), jnp.bfloat16),
            pltpu.VMEM((trade_n, SETS_DEV, width), jnp.float32),
            pltpu.VMEM((trade_n - 1, SETS_DEV, width), jnp.float32),
            pltpu.SemaphoreType.DMA,
            pltpu.SemaphoreType.DMA((chunks,)),
            pltpu.SemaphoreType.DMA,
            pltpu.SemaphoreType.DMA,
            pltpu.SemaphoreType.DMA,
            pltpu.SemaphoreType.DMA,
        ],
        compiler_params=pltpu.CompilerParams(
            collective_id=0, has_side_effects=True, vmem_limit_bytes=24 * 1024 * 1024
        ),
    )(
        row(initial_term_structure),
        row(long_level),
        row(reversion),
        row(volatility),
        mixing,
        shocks,
        cashflows,
        tall(maturity),
        tall(netting),
    )


def solution(mesh):
    return jax.shard_map(
        per_device,
        mesh=mesh,
        in_specs=(
            P(),
            P(),
            P(),
            P(),
            P(),
            P("date", None, None),
            P(None, "trade"),
            P("trade"),
            P("trade"),
        ),
        out_specs=P("date", "trade"),
        check_vma=False,
    )
```

```python
import functools

import jax
import jax.numpy as jnp
from jax import lax
from jax.experimental import pallas as pl
from jax.experimental.pallas import tpu as pltpu
from jax.sharding import PartitionSpec as P

SETS_DEV = 4
LANES = 128
MESH = pl.DeviceIdType.MESH


def each(count, body):
    if count <= 16:
        for index in range(count):
            body(index)
    else:
        pl.loop(0, count)(body)


def split(x):
    high = x.astype(jnp.bfloat16)
    low = (x - high.astype(jnp.float32)).astype(jnp.bfloat16)
    return high, low


def kernel(
    dates_dev,
    dates_n,
    trade_n,
    start_hbm,
    level_hbm,
    speed_hbm,
    vol_hbm,
    mixing_hbm,
    shocks_hbm,
    cash_hbm,
    maturity_hbm,
    netting_hbm,
    out_ref,
    start_ref,
    level_ref,
    speed_ref,
    vol_ref,
    mixing_ref,
    maturity_ref,
    netting_ref,
    shocks_v,
    cash_v,
    code_v,
    acc_v,
    offset_v,
    state_v,
    leave_v,
    arrive_v,
    send_v,
    recv_v,
    load_sem,
    cash_sem,
    leave_sem,
    arrive_sem,
    send_sem,
    recv_sem,
):
    factors, trades = cash_v.shape
    paths = shocks_v.shape[2]
    chunks = cash_sem.shape[0]
    chunk = trades // chunks
    sets_all = SETS_DEV * trade_n
    maturities = dates_dev * dates_n
    width = send_v.shape[2]
    date = lax.axis_index("date")
    me = lax.axis_index("trade")

    loads = [
        pltpu.make_async_copy(source, target, load_sem.at[place])
        for place, (source, target) in enumerate(
            (
                (shocks_hbm, shocks_v),
                (mixing_hbm, mixing_ref),
                (start_hbm, start_ref),
                (level_hbm, level_ref),
                (speed_hbm, speed_ref),
                (vol_hbm, vol_ref),
                (maturity_hbm, maturity_ref),
                (netting_hbm, netting_ref),
            )
        )
    ]
    for load in loads:
        load.start()

    def cash_copy(index):
        part = pl.ds(pl.multiple_of(index * chunk, chunk), chunk)
        return pltpu.make_async_copy(cash_hbm.at[:, part], cash_v.at[:, part], cash_sem.at[index])

    for index in range(chunks):
        cash_copy(index).start()

    barrier = pltpu.get_barrier_semaphore()

    def greet(index):
        other = lax.rem(me + 1 + index, trade_n)
        pl.semaphore_signal(barrier, inc=1, device_id={"trade": other}, device_id_type=MESH)

    each(trade_n - 1, greet)

    @pl.when(date > 0)
    def _():
        pl.semaphore_signal(barrier, inc=1, device_id={"date": date - 1}, device_id_type=MESH)

    for load in loads:
        load.wait()

    diagonal = lax.broadcasted_iota(jnp.int32, (factors, factors), 0) == lax.broadcasted_iota(
        jnp.int32, (factors, factors), 1
    )

    def column(ref):
        return jnp.sum(jnp.where(diagonal, ref[...], 0.0), axis=1, keepdims=True)

    decay = jnp.exp(-0.25 * column(speed_ref))
    drift = (1.0 - decay) * column(level_ref)
    start = jnp.broadcast_to(column(start_ref), (factors, paths))
    mix_high, mix_low = split(column(vol_ref) * mixing_ref[...])
    mix = jnp.concatenate([mix_high, mix_high, mix_low], axis=1)

    for m in range(1, maturities + 1):
        code_v[m - 1] = jnp.where(maturity_ref[...] == m, netting_ref[...], -1).astype(jnp.float32)

    running = None
    power = jnp.ones_like(decay)
    for step in range(dates_dev):
        high, low = split(shocks_v[step])
        moved = jnp.dot(
            mix, jnp.concatenate([high, low, high], axis=0), preferred_element_type=jnp.float32
        )
        running = drift + moved if step == 0 else decay * running + drift + moved
        power = power * decay
        offset_v[step] = running

    leave_copy = pltpu.make_async_remote_copy(
        src_ref=leave_v,
        dst_ref=arrive_v,
        send_sem=leave_sem,
        recv_sem=arrive_sem,
        device_id={"date": date + 1},
        device_id_type=MESH,
    )

    def leave(state):
        leave_v[...] = (power * state + running).astype(jnp.bfloat16)
        leave_copy.start()

    pl.semaphore_wait(barrier, trade_n - 1 + (date < dates_n - 1).astype(jnp.int32))

    @pl.when(date == 0)
    def _():
        state_v[...] = start
        leave(start)

    if dates_n > 2:

        @pl.when(jnp.logical_and(date > 0, date < dates_n - 1))
        def _():
            leave_copy.wait_recv()
            state = arrive_v[...].astype(jnp.float32)
            state_v[...] = state
            leave(state)

    tiles = sets_all // 16
    place = lax.broadcasted_iota(jnp.int32, (16, LANES), 0).astype(jnp.float32)
    marks = [(place + 16.0 * i).astype(jnp.bfloat16) for i in range(tiles)]
    one = jnp.ones((16, LANES), jnp.bfloat16)
    zero = jnp.zeros((16, LANES), jnp.bfloat16)
    rows = chunk // LANES

    def members(m, index):
        pieces = []
        for r in range(rows):
            code = jnp.broadcast_to(code_v[m, pl.ds(index * rows + r, 1), :], (16, LANES))
            code = code.astype(jnp.bfloat16)
            pieces.append(
                jnp.concatenate([jnp.where(code == mark, one, zero) for mark in marks], axis=0)
            )
        return jnp.concatenate(pieces, axis=1)

    def summed(member, index):
        cash = cash_v[:, pl.ds(pl.multiple_of(index * chunk, chunk), chunk)]
        cash = jnp.concatenate([cash] * dates_dev, axis=0)
        return lax.dot_general(
            member, cash, (((1,), (1,)), ((), ())), preferred_element_type=jnp.float32
        )

    lane = lax.broadcasted_iota(jnp.int32, (1, dates_dev * factors), 1)
    at_date = date * dates_dev + lane // factors

    def weight(m):
        return jnp.maximum(m - at_date, 0).astype(jnp.float32) / jnp.full_like(
            at_date, m
        ).astype(jnp.float32)

    if maturities * sets_all <= 256:
        total = jnp.zeros((maturities * sets_all, dates_dev * factors), jnp.float32)
        for index in range(chunks):
            cash_copy(index).wait()
            member = jnp.concatenate([members(m, index) for m in range(maturities)], axis=0)
            total = total + summed(member, index)
        held = jnp.zeros((sets_all, dates_dev * factors), jnp.float32)
        for m in range(maturities):
            held = held + weight(m + 1) * total[m * sets_all : (m + 1) * sets_all]
    else:
        acc_v[...] = jnp.zeros_like(acc_v)
        for index in range(chunks):
            cash_copy(index).wait()

        @pl.loop(0, chunks)
        def _(index):
            @pl.loop(0, maturities)
            def _(m):
                acc_v[...] += weight(m + 1) * summed(members(m, index), index)

        held = acc_v[...]

    send_v[...] = jnp.zeros_like(send_v)
    for owner in range(trade_n):
        send_v[owner, :, : dates_dev * factors] = held[owner * SETS_DEV : (owner + 1) * SETS_DEV]

    def push(index):
        other = lax.rem(me + 1 + index, trade_n)
        pltpu.make_async_remote_copy(
            src_ref=send_v.at[other],
            dst_ref=recv_v.at[index],
            send_sem=send_sem,
            recv_sem=recv_sem,
            device_id={"trade": other},
            device_id_type=MESH,
        ).start()

    each(trade_n - 1, push)

    @pl.when(date == dates_n - 1)
    def _():
        leave_copy.wait_recv()
        state_v[...] = arrive_v[...].astype(jnp.float32)

    tenor = 0.25 * (
        lax.broadcasted_iota(jnp.int32, (factors, 1), 0).astype(jnp.float32) + 1.0
    )
    discounts = []
    power = jnp.ones_like(decay)
    for step in range(dates_dev):
        power = power * decay
        now = power * state_v[...] + offset_v[step]
        discounts.append(jnp.exp(-now * tenor).astype(jnp.bfloat16))
    if width > dates_dev * factors:
        discounts.append(jnp.zeros((width - dates_dev * factors, paths), jnp.bfloat16))
    discount = jnp.concatenate(discounts, axis=0)

    everything = pltpu.make_async_copy(recv_v, recv_v, recv_sem)
    everything.wait()
    owned = send_v[me] + jnp.sum(recv_v[...], axis=0)
    lane = lax.broadcasted_iota(jnp.int32, owned.shape, 1) // factors
    owned = jnp.concatenate([jnp.where(lane == step, owned, 0.0) for step in range(dates_dev)], axis=0)
    high, low = split(owned)
    value = jnp.dot(high, discount, preferred_element_type=jnp.float32) + jnp.dot(
        low, discount, preferred_element_type=jnp.float32
    )
    mean = jnp.sum(jnp.maximum(value, 0.0), axis=1, keepdims=True) / paths
    pick = lax.broadcasted_iota(jnp.int32, (SETS_DEV, SETS_DEV), 0) == lax.broadcasted_iota(
        jnp.int32, (SETS_DEV, SETS_DEV), 1
    )
    for step in range(dates_dev):
        part = mean[step * SETS_DEV : (step + 1) * SETS_DEV]
        out_ref[step : step + 1, :] = jnp.sum(jnp.where(pick, part, 0.0), axis=0, keepdims=True)

    pltpu.make_async_copy(recv_v, recv_v, send_sem).wait()

    @pl.when(date < dates_n - 1)
    def _():
        leave_copy.wait_send()


def per_device(
    initial_term_structure,
    long_level,
    reversion,
    volatility,
    mixing,
    shocks,
    cashflows,
    maturity,
    netting,
):
    dates_dev, factors, paths = shocks.shape
    trades = cashflows.shape[1]
    dates_n = lax.axis_size("date")
    trade_n = lax.axis_size("trade")
    sets_all = SETS_DEV * trade_n
    width = -(-dates_dev * factors // LANES) * LANES
    chunks = max(1, trades // 1024)
    row = lambda x: x.reshape(1, factors)
    tall = lambda x: x.reshape(trades // LANES, LANES)
    vmem = pl.BlockSpec(memory_space=pltpu.VMEM)
    hbm = pl.BlockSpec(memory_space=pltpu.HBM)
    return pl.pallas_call(
        functools.partial(kernel, dates_dev, dates_n, trade_n),
        out_shape=jax.ShapeDtypeStruct((dates_dev, SETS_DEV), jnp.float32),
        in_specs=[hbm] * 9,
        out_specs=vmem,
        scratch_shapes=[
            pltpu.VMEM((1, factors), jnp.float32),
            pltpu.VMEM((1, factors), jnp.float32),
            pltpu.VMEM((1, factors), jnp.float32),
            pltpu.VMEM((1, factors), jnp.float32),
            pltpu.VMEM((factors, factors), jnp.float32),
            pltpu.VMEM((trades // LANES, LANES), jnp.int32),
            pltpu.VMEM((trades // LANES, LANES), jnp.int32),
            pltpu.VMEM((dates_dev, factors, paths), jnp.float32),
            pltpu.VMEM((factors, trades), jnp.bfloat16),
            pltpu.VMEM((dates_dev * dates_n, trades // LANES, LANES), jnp.float32),
            pltpu.VMEM((sets_all, dates_dev * factors), jnp.float32),
            pltpu.VMEM((dates_dev, factors, paths), jnp.float32),
            pltpu.VMEM((factors, paths), jnp.float32),
            pltpu.VMEM((factors, paths), jnp.bfloat16),
            pltpu.VMEM((factors, paths), jnp.bfloat16),
            pltpu.VMEM((trade_n, SETS_DEV, width), jnp.float32),
            pltpu.VMEM((trade_n - 1, SETS_DEV, width), jnp.float32),
            pltpu.SemaphoreType.DMA((8,)),
            pltpu.SemaphoreType.DMA((chunks,)),
            pltpu.SemaphoreType.DMA,
            pltpu.SemaphoreType.DMA,
            pltpu.SemaphoreType.DMA,
            pltpu.SemaphoreType.DMA,
        ],
        compiler_params=pltpu.CompilerParams(
            collective_id=0, has_side_effects=True, vmem_limit_bytes=24 * 1024 * 1024
        ),
    )(
        row(initial_term_structure),
        row(long_level),
        row(reversion),
        row(volatility),
        mixing,
        shocks,
        cashflows,
        tall(maturity),
        tall(netting),
    )


def solution(mesh):
    return jax.shard_map(
        per_device,
        mesh=mesh,
        in_specs=(
            P(),
            P(),
            P(),
            P(),
            P(),
            P("date", None, None),
            P(None, "trade"),
            P("trade"),
            P("trade"),
        ),
        out_specs=P("date", "trade"),
        check_vma=False,
    )
```

```python
import functools

import jax
import jax.numpy as jnp
from jax import lax
from jax.experimental import pallas as pl
from jax.experimental.pallas import tpu as pltpu
from jax.sharding import PartitionSpec as P

SETS_DEV = 4
LANES = 128
MESH = pl.DeviceIdType.MESH


def each(count, body):
    if count <= 16:
        for index in range(count):
            body(index)
    else:
        pl.loop(0, count)(body)


def split(x):
    high = x.astype(jnp.bfloat16)
    low = (x - high.astype(jnp.float32)).astype(jnp.bfloat16)
    return high, low


def kernel(
    dates_dev,
    dates_n,
    trade_n,
    start_hbm,
    level_hbm,
    speed_hbm,
    vol_hbm,
    mixing_hbm,
    shocks_hbm,
    cash_hbm,
    maturity_hbm,
    netting_hbm,
    out_ref,
    start_ref,
    level_ref,
    speed_ref,
    vol_ref,
    mixing_ref,
    maturity_ref,
    netting_ref,
    shocks_v,
    cash_v,
    code_v,
    acc_v,
    offset_v,
    state_v,
    leave_v,
    arrive_v,
    send_v,
    recv_v,
    load_sem,
    cash_sem,
    leave_sem,
    arrive_sem,
    send_sem,
    recv_sem,
):
    factors, trades = cash_v.shape
    paths = shocks_v.shape[2]
    chunks = cash_sem.shape[0]
    chunk = trades // chunks
    sets_all = SETS_DEV * trade_n
    maturities = dates_dev * dates_n
    width = send_v.shape[2]
    date = lax.axis_index("date")
    me = lax.axis_index("trade")

    loads = [
        pltpu.make_async_copy(source, target, load_sem.at[place])
        for place, (source, target) in enumerate(
            (
                (shocks_hbm, shocks_v),
                (mixing_hbm, mixing_ref),
                (start_hbm, start_ref),
                (level_hbm, level_ref),
                (speed_hbm, speed_ref),
                (vol_hbm, vol_ref),
                (maturity_hbm, maturity_ref),
                (netting_hbm, netting_ref),
            )
        )
    ]
    for load in loads:
        load.start()

    def cash_copy(index):
        part = pl.ds(pl.multiple_of(index * chunk, chunk), chunk)
        return pltpu.make_async_copy(cash_hbm.at[:, part], cash_v.at[:, part], cash_sem.at[index])

    for index in range(chunks):
        cash_copy(index).start()

    barrier = pltpu.get_barrier_semaphore()

    def greet(index):
        other = lax.rem(me + 1 + index, trade_n)
        pl.semaphore_signal(barrier, inc=1, device_id={"trade": other}, device_id_type=MESH)

    each(trade_n - 1, greet)

    @pl.when(date > 0)
    def _():
        pl.semaphore_signal(barrier, inc=1, device_id={"date": date - 1}, device_id_type=MESH)

    for load in loads:
        load.wait()

    diagonal = lax.broadcasted_iota(jnp.int32, (factors, factors), 0) == lax.broadcasted_iota(
        jnp.int32, (factors, factors), 1
    )

    def column(ref):
        return jnp.sum(jnp.where(diagonal, ref[...], 0.0), axis=1, keepdims=True)

    decay = jnp.exp(-0.25 * column(speed_ref))
    drift = (1.0 - decay) * column(level_ref)
    start = jnp.broadcast_to(column(start_ref), (factors, paths))
    mix_high, mix_low = split(column(vol_ref) * mixing_ref[...])
    mix = jnp.concatenate([mix_high, mix_high, mix_low], axis=1)

    for m in range(1, maturities + 1):
        code_v[m - 1] = jnp.where(maturity_ref[...] == m, netting_ref[...], -1).astype(jnp.float32)

    running = None
    power = jnp.ones_like(decay)
    for step in range(dates_dev):
        high, low = split(shocks_v[step])
        moved = jnp.dot(
            mix, jnp.concatenate([high, low, high], axis=0), preferred_element_type=jnp.float32
        )
        running = drift + moved if step == 0 else decay * running + drift + moved
        power = power * decay
        offset_v[step] = running

    leave_copy = pltpu.make_async_remote_copy(
        src_ref=leave_v,
        dst_ref=arrive_v,
        send_sem=leave_sem,
        recv_sem=arrive_sem,
        device_id={"date": date + 1},
        device_id_type=MESH,
    )

    def leave(state):
        leave_v[...] = (power * state + running).astype(jnp.bfloat16)
        leave_copy.start()

    pl.semaphore_wait(barrier, trade_n - 1 + (date < dates_n - 1).astype(jnp.int32))

    @pl.when(date == 0)
    def _():
        state_v[...] = start
        leave(start)

    if dates_n > 2:

        @pl.when(jnp.logical_and(date > 0, date < dates_n - 1))
        def _():
            leave_copy.wait_recv()
            state = arrive_v[...].astype(jnp.float32)
            state_v[...] = state
            leave(state)

    tiles = sets_all // 16
    place = lax.broadcasted_iota(jnp.int32, (16, LANES), 0).astype(jnp.float32)
    marks = [(place + 16.0 * i).astype(jnp.bfloat16) for i in range(tiles)]
    one = jnp.ones((16, LANES), jnp.bfloat16)
    zero = jnp.zeros((16, LANES), jnp.bfloat16)
    rows = chunk // LANES

    def members(m, index):
        pieces = []
        for r in range(rows):
            code = jnp.broadcast_to(code_v[m, pl.ds(index * rows + r, 1), :], (16, LANES))
            code = code.astype(jnp.bfloat16)
            pieces.append(
                jnp.concatenate([jnp.where(code == mark, one, zero) for mark in marks], axis=0)
            )
        return jnp.concatenate(pieces, axis=1)

    def summed(member, index):
        cash = cash_v[:, pl.ds(pl.multiple_of(index * chunk, chunk), chunk)]
        cash = jnp.concatenate([cash] * dates_dev, axis=0)
        return lax.dot_general(
            member, cash, (((1,), (1,)), ((), ())), preferred_element_type=jnp.float32
        )

    lane = lax.broadcasted_iota(jnp.int32, (1, dates_dev * factors), 1)
    at_date = date * dates_dev + lane // factors

    def weight(m):
        return jnp.maximum(m - at_date, 0).astype(jnp.float32) / jnp.full_like(
            at_date, m
        ).astype(jnp.float32)

    if maturities * sets_all <= 256:
        total = jnp.zeros((maturities * sets_all, dates_dev * factors), jnp.float32)
        for index in range(chunks):
            cash_copy(index).wait()
            member = jnp.concatenate([members(m, index) for m in range(maturities)], axis=0)
            total = total + summed(member, index)
        held = jnp.zeros((sets_all, dates_dev * factors), jnp.float32)
        for m in range(maturities):
            held = held + weight(m + 1) * total[m * sets_all : (m + 1) * sets_all]
    else:
        acc_v[...] = jnp.zeros_like(acc_v)
        for index in range(chunks):
            cash_copy(index).wait()

        @pl.loop(0, chunks)
        def _(index):
            @pl.loop(0, maturities)
            def _(m):
                acc_v[...] += weight(m + 1) * summed(members(m, index), index)

        held = acc_v[...]

    send_v[...] = jnp.zeros_like(send_v)
    for owner in range(trade_n):
        send_v[owner, :, : dates_dev * factors] = held[owner * SETS_DEV : (owner + 1) * SETS_DEV]

    def push(index):
        other = lax.rem(me + 1 + index, trade_n)
        pltpu.make_async_remote_copy(
            src_ref=send_v.at[other],
            dst_ref=recv_v.at[index],
            send_sem=send_sem,
            recv_sem=recv_sem,
            device_id={"trade": other},
            device_id_type=MESH,
        ).start()

    each(trade_n - 1, push)

    @pl.when(date == dates_n - 1)
    def _():
        leave_copy.wait_recv()
        state_v[...] = arrive_v[...].astype(jnp.float32)

    tenor = 0.25 * (
        lax.broadcasted_iota(jnp.int32, (factors, 1), 0).astype(jnp.float32) + 1.0
    )
    discounts = []
    power = jnp.ones_like(decay)
    for step in range(dates_dev):
        power = power * decay
        now = power * state_v[...] + offset_v[step]
        discounts.append(jnp.exp(-now * tenor).astype(jnp.bfloat16))
    if width > dates_dev * factors:
        discounts.append(jnp.zeros((width - dates_dev * factors, paths), jnp.bfloat16))
    discount = jnp.concatenate(discounts, axis=0)

    everything = pltpu.make_async_copy(recv_v, recv_v, recv_sem)
    everything.wait()
    owned = send_v[me] + jnp.sum(recv_v[...], axis=0)
    lane = lax.broadcasted_iota(jnp.int32, owned.shape, 1) // factors
    owned = jnp.concatenate([jnp.where(lane == step, owned, 0.0) for step in range(dates_dev)], axis=0)
    high, low = split(owned)
    value = jnp.dot(high, discount, preferred_element_type=jnp.float32) + jnp.dot(
        low, discount, preferred_element_type=jnp.float32
    )
    mean = jnp.sum(jnp.maximum(value, 0.0), axis=1, keepdims=True) / paths
    pick = lax.broadcasted_iota(jnp.int32, (SETS_DEV, SETS_DEV), 0) == lax.broadcasted_iota(
        jnp.int32, (SETS_DEV, SETS_DEV), 1
    )
    for step in range(dates_dev):
        part = mean[step * SETS_DEV : (step + 1) * SETS_DEV]
        out_ref[step : step + 1, :] = jnp.sum(jnp.where(pick, part, 0.0), axis=0, keepdims=True)

    pltpu.make_async_copy(recv_v, recv_v, send_sem).wait()

    @pl.when(date < dates_n - 1)
    def _():
        leave_copy.wait_send()


def per_device(
    initial_term_structure,
    long_level,
    reversion,
    volatility,
    mixing,
    shocks,
    cashflows,
    maturity,
    netting,
):
    dates_dev, factors, paths = shocks.shape
    trades = cashflows.shape[1]
    dates_n = lax.axis_size("date")
    trade_n = lax.axis_size("trade")
    sets_all = SETS_DEV * trade_n
    width = -(-dates_dev * factors // LANES) * LANES
    chunks = max(1, trades // 1024)
    row = lambda x: x.reshape(1, factors)
    tall = lambda x: x.reshape(trades // LANES, LANES)
    vmem = pl.BlockSpec(memory_space=pltpu.VMEM)
    hbm = pl.BlockSpec(memory_space=pltpu.HBM)
    return pl.pallas_call(
        functools.partial(kernel, dates_dev, dates_n, trade_n),
        out_shape=jax.ShapeDtypeStruct((dates_dev, SETS_DEV), jnp.float32),
        in_specs=[hbm] * 9,
        out_specs=vmem,
        scratch_shapes=[
            pltpu.VMEM((1, factors), jnp.float32),
            pltpu.VMEM((1, factors), jnp.float32),
            pltpu.VMEM((1, factors), jnp.float32),
            pltpu.VMEM((1, factors), jnp.float32),
            pltpu.VMEM((factors, factors), jnp.float32),
            pltpu.VMEM((trades // LANES, LANES), jnp.int32),
            pltpu.VMEM((trades // LANES, LANES), jnp.int32),
            pltpu.VMEM((dates_dev, factors, paths), jnp.float32),
            pltpu.VMEM((factors, trades), jnp.bfloat16),
            pltpu.VMEM((dates_dev * dates_n, trades // LANES, LANES), jnp.float32),
            pltpu.VMEM((sets_all, dates_dev * factors), jnp.float32),
            pltpu.VMEM((dates_dev, factors, paths), jnp.float32),
            pltpu.VMEM((factors, paths), jnp.float32),
            pltpu.VMEM((factors, paths), jnp.bfloat16),
            pltpu.VMEM((factors, paths), jnp.bfloat16),
            pltpu.VMEM((trade_n, SETS_DEV, width), jnp.float32),
            pltpu.VMEM((trade_n - 1, SETS_DEV, width), jnp.float32),
            pltpu.SemaphoreType.DMA((8,)),
            pltpu.SemaphoreType.DMA((chunks,)),
            pltpu.SemaphoreType.DMA,
            pltpu.SemaphoreType.DMA,
            pltpu.SemaphoreType.DMA,
            pltpu.SemaphoreType.DMA,
        ],
        compiler_params=pltpu.CompilerParams(
            collective_id=0, has_side_effects=True, vmem_limit_bytes=60 * 1024 * 1024
        ),
    )(
        row(initial_term_structure),
        row(long_level),
        row(reversion),
        row(volatility),
        mixing,
        shocks,
        cashflows,
        tall(maturity),
        tall(netting),
    )


def solution(mesh):
    return jax.shard_map(
        per_device,
        mesh=mesh,
        in_specs=(
            P(),
            P(),
            P(),
            P(),
            P(),
            P("date", None, None),
            P(None, "trade"),
            P("trade"),
            P("trade"),
        ),
        out_specs=P("date", "trade"),
        check_vma=False,
    )
```

```python
import functools
import math

import jax
import jax.numpy as jnp
from jax import lax
from jax.experimental import pallas as pl
from jax.experimental.pallas import tpu as pltpu
from jax.sharding import PartitionSpec as P

SETS_DEV = 4
LANES = 128
MESH = pl.DeviceIdType.MESH


def each(count, body):
    if count <= 16:
        for index in range(count):
            body(index)
    else:
        pl.loop(0, count)(body)


def split(x):
    high = x.astype(jnp.bfloat16)
    low = (x - high.astype(jnp.float32)).astype(jnp.bfloat16)
    return high, low


def kernel(
    dates_dev,
    dates_n,
    trade_n,
    start_hbm,
    level_hbm,
    speed_hbm,
    vol_hbm,
    mixing_hbm,
    shocks_hbm,
    cash_hbm,
    maturity_hbm,
    netting_hbm,
    out_ref,
    start_ref,
    level_ref,
    speed_ref,
    vol_ref,
    mixing_ref,
    maturity_ref,
    netting_ref,
    shocks_v,
    cash_v,
    code_v,
    acc_v,
    offset_v,
    state_v,
    leave_v,
    arrive_v,
    send_v,
    recv_v,
    load_sem,
    cash_sem,
    leave_sem,
    arrive_sem,
    send_sem,
    recv_sem,
):
    factors, trades = cash_v.shape
    paths = shocks_v.shape[2]
    chunks = cash_sem.shape[0]
    chunk = trades // chunks
    sets_all = SETS_DEV * trade_n
    maturities = dates_dev * dates_n
    width = send_v.shape[2]
    date = lax.axis_index("date")
    me = lax.axis_index("trade")

    loads = [
        pltpu.make_async_copy(source, target, load_sem.at[place])
        for place, (source, target) in enumerate(
            (
                (shocks_hbm, shocks_v),
                (mixing_hbm, mixing_ref),
                (start_hbm, start_ref),
                (level_hbm, level_ref),
                (speed_hbm, speed_ref),
                (vol_hbm, vol_ref),
                (maturity_hbm, maturity_ref),
                (netting_hbm, netting_ref),
            )
        )
    ]
    for load in loads:
        load.start()

    def cash_copy(index):
        part = pl.ds(pl.multiple_of(index * chunk, chunk), chunk)
        return pltpu.make_async_copy(cash_hbm.at[:, part], cash_v.at[:, part], cash_sem.at[index])

    for index in range(chunks):
        cash_copy(index).start()

    barrier = pltpu.get_barrier_semaphore()

    def greet(index):
        other = lax.rem(me + 1 + index, trade_n)
        pl.semaphore_signal(barrier, inc=1, device_id={"trade": other}, device_id_type=MESH)

    each(trade_n - 1, greet)

    @pl.when(date > 0)
    def _():
        pl.semaphore_signal(barrier, inc=1, device_id={"date": date - 1}, device_id_type=MESH)

    for load in loads:
        load.wait()

    diagonal = lax.broadcasted_iota(jnp.int32, (factors, factors), 0) == lax.broadcasted_iota(
        jnp.int32, (factors, factors), 1
    )

    def column(ref):
        return jnp.sum(jnp.where(diagonal, ref[...], 0.0), axis=1, keepdims=True)

    decay = jnp.exp(-0.25 * column(speed_ref))
    drift = (1.0 - decay) * column(level_ref)
    start = jnp.broadcast_to(column(start_ref), (factors, paths))
    mix_high, mix_low = split(column(vol_ref) * mixing_ref[...])
    mix = jnp.concatenate([mix_high, mix_high, mix_low], axis=1)

    common = math.lcm(*range(1, maturities + 1))
    whole = common <= 256
    if whole:
        expiry = maturity_ref[...]
        share = jnp.zeros_like(expiry)
        for m in range(1, maturities + 1):
            share = jnp.where(expiry == m, common // m, share)
        code_v[dates_dev] = netting_ref[...].astype(jnp.float32)
        for step in range(dates_dev):
            left = jnp.maximum(expiry - (date * dates_dev + step), 0)
            code_v[step] = (share * left).astype(jnp.float32)
    else:
        for m in range(1, maturities + 1):
            code_v[m - 1] = jnp.where(maturity_ref[...] == m, netting_ref[...], -1).astype(
                jnp.float32
            )

    running = None
    power = jnp.ones_like(decay)
    for step in range(dates_dev):
        high, low = split(shocks_v[step])
        moved = jnp.dot(
            mix, jnp.concatenate([high, low, high], axis=0), preferred_element_type=jnp.float32
        )
        running = drift + moved if step == 0 else decay * running + drift + moved
        power = power * decay
        offset_v[step] = running

    leave_copy = pltpu.make_async_remote_copy(
        src_ref=leave_v,
        dst_ref=arrive_v,
        send_sem=leave_sem,
        recv_sem=arrive_sem,
        device_id={"date": date + 1},
        device_id_type=MESH,
    )

    def leave(state):
        leave_v[...] = (power * state + running).astype(jnp.bfloat16)
        leave_copy.start()

    tiles = sets_all // 16
    place = lax.broadcasted_iota(jnp.int32, (16, LANES), 0).astype(jnp.float32)
    marks = [(place + 16.0 * i).astype(jnp.bfloat16) for i in range(tiles)]
    one = jnp.ones((16, LANES), jnp.bfloat16)
    zero = jnp.zeros((16, LANES), jnp.bfloat16)
    rows = chunk // LANES

    def members(m, index):
        pieces = []
        for r in range(rows):
            code = jnp.broadcast_to(code_v[m, pl.ds(index * rows + r, 1), :], (16, LANES))
            code = code.astype(jnp.bfloat16)
            pieces.append(
                jnp.concatenate([jnp.where(code == mark, one, zero) for mark in marks], axis=0)
            )
        return jnp.concatenate(pieces, axis=1)

    def weighted(index):
        pieces = []
        for r in range(rows):
            spread = [
                jnp.broadcast_to(
                    code_v[step, pl.ds(index * rows + r, 1), :], (16, LANES)
                ).astype(jnp.bfloat16)
                for step in range(dates_dev + 1)
            ]
            same = [spread[-1] == mark for mark in marks]
            pieces.append(
                jnp.concatenate(
                    [jnp.where(here, share, zero) for share in spread[:-1] for here in same], axis=0
                )
            )
        return jnp.concatenate(pieces, axis=1)

    def summed(member, index, copies):
        cash = cash_v[:, pl.ds(pl.multiple_of(index * chunk, chunk), chunk)]
        cash = jnp.concatenate([cash] * copies, axis=0)
        return lax.dot_general(
            member, cash, (((1,), (1,)), ((), ())), preferred_element_type=jnp.float32
        )

    lane = lax.broadcasted_iota(jnp.int32, (1, dates_dev * factors), 1)
    at_date = date * dates_dev + lane // factors

    def weight(m):
        return jnp.maximum(m - at_date, 0).astype(jnp.float32) / jnp.full_like(
            at_date, m
        ).astype(jnp.float32)

    if whole:
        total = jnp.zeros((dates_dev * sets_all, factors), jnp.float32)
        for index in range(chunks):
            cash_copy(index).wait()
            total = total + summed(weighted(index), index, 1)
        total = total * (1.0 / common)
        held = jnp.concatenate(
            [total[step * sets_all : (step + 1) * sets_all] for step in range(dates_dev)], axis=1
        )
    else:
        acc_v[...] = jnp.zeros_like(acc_v)
        for index in range(chunks):
            cash_copy(index).wait()

        @pl.loop(0, chunks)
        def _(index):
            @pl.loop(0, maturities)
            def _(m):
                acc_v[...] += weight(m + 1) * summed(members(m, index), index, dates_dev)

        held = acc_v[...]

    send_v[...] = jnp.zeros_like(send_v)
    for owner in range(trade_n):
        send_v[owner, :, : dates_dev * factors] = held[owner * SETS_DEV : (owner + 1) * SETS_DEV]

    pl.semaphore_wait(barrier, trade_n - 1 + (date < dates_n - 1).astype(jnp.int32))

    @pl.when(date == 0)
    def _():
        state_v[...] = start
        leave(start)

    if dates_n > 2:

        @pl.when(jnp.logical_and(date > 0, date < dates_n - 1))
        def _():
            leave_copy.wait_recv()
            state = arrive_v[...].astype(jnp.float32)
            state_v[...] = state
            leave(state)

    def push(index):
        other = index + (index >= me).astype(jnp.int32)
        pltpu.make_async_remote_copy(
            src_ref=send_v.at[other],
            dst_ref=recv_v.at[me - (me > other).astype(jnp.int32)],
            send_sem=send_sem,
            recv_sem=recv_sem,
            device_id={"trade": other},
            device_id_type=MESH,
        ).start()

    each(trade_n - 1, push)

    @pl.when(date == dates_n - 1)
    def _():
        leave_copy.wait_recv()
        state_v[...] = arrive_v[...].astype(jnp.float32)

    tenor = 0.25 * (
        lax.broadcasted_iota(jnp.int32, (factors, 1), 0).astype(jnp.float32) + 1.0
    )
    discounts = []
    power = jnp.ones_like(decay)
    for step in range(dates_dev):
        power = power * decay
        now = power * state_v[...] + offset_v[step]
        discounts.append(jnp.exp(-now * tenor).astype(jnp.bfloat16))
    if width > dates_dev * factors:
        discounts.append(jnp.zeros((width - dates_dev * factors, paths), jnp.bfloat16))
    discount = jnp.concatenate(discounts, axis=0)

    everything = pltpu.make_async_copy(recv_v, recv_v, recv_sem)
    everything.wait()
    owned = send_v[me] + jnp.sum(recv_v[...], axis=0)
    lane = lax.broadcasted_iota(jnp.int32, owned.shape, 1) // factors
    owned = jnp.concatenate([jnp.where(lane == step, owned, 0.0) for step in range(dates_dev)], axis=0)
    high, low = split(owned)
    value = jnp.dot(high, discount, preferred_element_type=jnp.float32) + jnp.dot(
        low, discount, preferred_element_type=jnp.float32
    )
    mean = jnp.sum(jnp.maximum(value, 0.0), axis=1, keepdims=True) / paths
    pick = lax.broadcasted_iota(jnp.int32, (SETS_DEV, SETS_DEV), 0) == lax.broadcasted_iota(
        jnp.int32, (SETS_DEV, SETS_DEV), 1
    )
    for step in range(dates_dev):
        part = mean[step * SETS_DEV : (step + 1) * SETS_DEV]
        out_ref[step : step + 1, :] = jnp.sum(jnp.where(pick, part, 0.0), axis=0, keepdims=True)

    pltpu.make_async_copy(recv_v, recv_v, send_sem).wait()

    @pl.when(date < dates_n - 1)
    def _():
        leave_copy.wait_send()


def per_device(
    initial_term_structure,
    long_level,
    reversion,
    volatility,
    mixing,
    shocks,
    cashflows,
    maturity,
    netting,
):
    dates_dev, factors, paths = shocks.shape
    trades = cashflows.shape[1]
    dates_n = lax.axis_size("date")
    trade_n = lax.axis_size("trade")
    sets_all = SETS_DEV * trade_n
    width = -(-dates_dev * factors // LANES) * LANES
    chunks = max(1, trades // 2048)
    row = lambda x: x.reshape(1, factors)
    tall = lambda x: x.reshape(trades // LANES, LANES)
    keep = lambda x: pltpu.with_memory_space_constraint(x, pltpu.HBM)
    vmem = pl.BlockSpec(memory_space=pltpu.VMEM)
    hbm = pl.BlockSpec(memory_space=pltpu.HBM)
    return pl.pallas_call(
        functools.partial(kernel, dates_dev, dates_n, trade_n),
        out_shape=jax.ShapeDtypeStruct((dates_dev, SETS_DEV), jnp.float32),
        in_specs=[hbm] * 9,
        out_specs=vmem,
        scratch_shapes=[
            pltpu.VMEM((1, factors), jnp.float32),
            pltpu.VMEM((1, factors), jnp.float32),
            pltpu.VMEM((1, factors), jnp.float32),
            pltpu.VMEM((1, factors), jnp.float32),
            pltpu.VMEM((factors, factors), jnp.float32),
            pltpu.VMEM((trades // LANES, LANES), jnp.int32),
            pltpu.VMEM((trades // LANES, LANES), jnp.int32),
            pltpu.VMEM((dates_dev, factors, paths), jnp.float32),
            pltpu.VMEM((factors, trades), jnp.bfloat16),
            pltpu.VMEM((max(dates_dev + 1, dates_dev * dates_n), trades // LANES, LANES), jnp.float32),
            pltpu.VMEM((sets_all, dates_dev * factors), jnp.float32),
            pltpu.VMEM((dates_dev, factors, paths), jnp.float32),
            pltpu.VMEM((factors, paths), jnp.float32),
            pltpu.VMEM((factors, paths), jnp.bfloat16),
            pltpu.VMEM((factors, paths), jnp.bfloat16),
            pltpu.VMEM((trade_n, SETS_DEV, width), jnp.float32),
            pltpu.VMEM((trade_n - 1, SETS_DEV, width), jnp.float32),
            pltpu.SemaphoreType.DMA((8,)),
            pltpu.SemaphoreType.DMA((chunks,)),
            pltpu.SemaphoreType.DMA,
            pltpu.SemaphoreType.DMA,
            pltpu.SemaphoreType.DMA,
            pltpu.SemaphoreType.DMA,
        ],
        compiler_params=pltpu.CompilerParams(
            collective_id=0, has_side_effects=True, vmem_limit_bytes=24 * 1024 * 1024
        ),
    )(
        keep(row(initial_term_structure)),
        keep(row(long_level)),
        keep(row(reversion)),
        keep(row(volatility)),
        keep(mixing),
        keep(shocks),
        keep(cashflows),
        keep(tall(maturity)),
        keep(tall(netting)),
    )


def solution(mesh):
    return jax.shard_map(
        per_device,
        mesh=mesh,
        in_specs=(
            P(),
            P(),
            P(),
            P(),
            P(),
            P("date", None, None),
            P(None, "trade"),
            P("trade"),
            P("trade"),
        ),
        out_specs=P("date", "trade"),
        check_vma=False,
    )
```

```python
import functools
import math

import jax
import jax.numpy as jnp
from jax import lax
from jax.experimental import pallas as pl
from jax.experimental.pallas import tpu as pltpu
from jax.sharding import PartitionSpec as P

SETS_DEV = 4
LANES = 128
MESH = pl.DeviceIdType.MESH


def each(count, body):
    if count <= 16:
        for index in range(count):
            body(index)
    else:
        pl.loop(0, count)(body)


def split(x):
    high = x.astype(jnp.bfloat16)
    low = (x - high.astype(jnp.float32)).astype(jnp.bfloat16)
    return high, low


def kernel(
    dates_dev,
    dates_n,
    trade_n,
    start_hbm,
    level_hbm,
    speed_hbm,
    vol_hbm,
    mixing_hbm,
    shocks_hbm,
    cash_hbm,
    maturity_hbm,
    netting_hbm,
    out_ref,
    start_ref,
    level_ref,
    speed_ref,
    vol_ref,
    mixing_ref,
    maturity_ref,
    netting_ref,
    shocks_v,
    cash_v,
    code_v,
    acc_v,
    offset_v,
    state_v,
    leave_v,
    arrive_v,
    send_v,
    recv_v,
    load_sem,
    cash_sem,
    leave_sem,
    arrive_sem,
    send_sem,
    recv_sem,
):
    factors, trades = cash_v.shape
    paths = shocks_v.shape[2]
    chunks = cash_sem.shape[0]
    chunk = trades // chunks
    sets_all = SETS_DEV * trade_n
    maturities = dates_dev * dates_n
    width = send_v.shape[2]
    date = lax.axis_index("date")
    me = lax.axis_index("trade")

    loads = [
        pltpu.make_async_copy(source, target, load_sem.at[place])
        for place, (source, target) in enumerate(
            (
                (shocks_hbm, shocks_v),
                (mixing_hbm, mixing_ref),
                (start_hbm, start_ref),
                (level_hbm, level_ref),
                (speed_hbm, speed_ref),
                (vol_hbm, vol_ref),
                (maturity_hbm, maturity_ref),
                (netting_hbm, netting_ref),
            )
        )
    ]
    for load in loads:
        load.start()

    def cash_copy(index):
        part = pl.ds(pl.multiple_of(index * chunk, chunk), chunk)
        return pltpu.make_async_copy(cash_hbm.at[:, part], cash_v.at[:, part], cash_sem.at[index])

    for index in range(chunks):
        cash_copy(index).start()

    barrier = pltpu.get_barrier_semaphore()

    def greet(index):
        other = lax.rem(me + 1 + index, trade_n)
        pl.semaphore_signal(barrier, inc=1, device_id={"trade": other}, device_id_type=MESH)

    each(trade_n - 1, greet)

    @pl.when(date > 0)
    def _():
        pl.semaphore_signal(barrier, inc=1, device_id={"date": date - 1}, device_id_type=MESH)

    for load in loads:
        load.wait()

    diagonal = lax.broadcasted_iota(jnp.int32, (factors, factors), 0) == lax.broadcasted_iota(
        jnp.int32, (factors, factors), 1
    )

    def column(ref):
        return jnp.sum(jnp.where(diagonal, ref[...], 0.0), axis=1, keepdims=True)

    decay = jnp.exp(-0.25 * column(speed_ref))
    drift = (1.0 - decay) * column(level_ref)
    start = jnp.broadcast_to(column(start_ref), (factors, paths))
    mix_high, mix_low = split(column(vol_ref) * mixing_ref[...])
    mix = jnp.concatenate([mix_high, mix_high, mix_low], axis=1)

    common = math.lcm(*range(1, maturities + 1))
    whole = common <= 256
    if whole:
        expiry = maturity_ref[...]
        share = jnp.zeros_like(expiry)
        for m in range(1, maturities + 1):
            share = jnp.where(expiry == m, common // m, share)
        code_v[dates_dev] = netting_ref[...].astype(jnp.float32)
        for step in range(dates_dev):
            left = jnp.maximum(expiry - (date * dates_dev + step), 0)
            code_v[step] = (share * left).astype(jnp.float32)
    else:
        for m in range(1, maturities + 1):
            code_v[m - 1] = jnp.where(maturity_ref[...] == m, netting_ref[...], -1).astype(
                jnp.float32
            )

    running = None
    power = jnp.ones_like(decay)
    for step in range(dates_dev):
        high, low = split(shocks_v[step])
        moved = jnp.dot(
            mix, jnp.concatenate([high, low, high], axis=0), preferred_element_type=jnp.float32
        )
        running = drift + moved if step == 0 else decay * running + drift + moved
        power = power * decay
        offset_v[step] = running

    leave_copy = pltpu.make_async_remote_copy(
        src_ref=leave_v,
        dst_ref=arrive_v,
        send_sem=leave_sem,
        recv_sem=arrive_sem,
        device_id={"date": date + 1},
        device_id_type=MESH,
    )

    def leave(state):
        leave_v[...] = (power * state + running).astype(jnp.bfloat16)
        leave_copy.start()

    tiles = sets_all // 16
    place = lax.broadcasted_iota(jnp.int32, (16, LANES), 0).astype(jnp.float32)
    marks = [(place + 16.0 * i).astype(jnp.bfloat16) for i in range(tiles)]
    one = jnp.ones((16, LANES), jnp.bfloat16)
    zero = jnp.zeros((16, LANES), jnp.bfloat16)
    rows = chunk // LANES

    def members(m, index):
        pieces = []
        for r in range(rows):
            code = jnp.broadcast_to(code_v[m, pl.ds(index * rows + r, 1), :], (16, LANES))
            code = code.astype(jnp.bfloat16)
            pieces.append(
                jnp.concatenate([jnp.where(code == mark, one, zero) for mark in marks], axis=0)
            )
        return jnp.concatenate(pieces, axis=1)

    def weighted(index):
        pieces = []
        for r in range(rows):
            spread = [
                jnp.broadcast_to(
                    code_v[step, pl.ds(index * rows + r, 1), :], (16, LANES)
                ).astype(jnp.bfloat16)
                for step in range(dates_dev + 1)
            ]
            same = [spread[-1] == mark for mark in marks]
            pieces.append(
                jnp.concatenate(
                    [jnp.where(here, share, zero) for share in spread[:-1] for here in same], axis=0
                )
            )
        return jnp.concatenate(pieces, axis=1)

    def summed(member, index, copies):
        cash = cash_v[:, pl.ds(pl.multiple_of(index * chunk, chunk), chunk)]
        cash = jnp.concatenate([cash] * copies, axis=0)
        return lax.dot_general(
            member, cash, (((1,), (1,)), ((), ())), preferred_element_type=jnp.float32
        )

    lane = lax.broadcasted_iota(jnp.int32, (1, dates_dev * factors), 1)
    at_date = date * dates_dev + lane // factors

    def weight(m):
        return jnp.maximum(m - at_date, 0).astype(jnp.float32) / jnp.full_like(
            at_date, m
        ).astype(jnp.float32)

    if whole:
        total = jnp.zeros((dates_dev * sets_all, factors), jnp.float32)
        for index in range(chunks):
            cash_copy(index).wait()
            total = total + summed(weighted(index), index, 1)
        total = total * (1.0 / common)
        held = jnp.concatenate(
            [total[step * sets_all : (step + 1) * sets_all] for step in range(dates_dev)], axis=1
        )
    else:
        acc_v[...] = jnp.zeros_like(acc_v)
        for index in range(chunks):
            cash_copy(index).wait()

        @pl.loop(0, chunks)
        def _(index):
            @pl.loop(0, maturities)
            def _(m):
                acc_v[...] += weight(m + 1) * summed(members(m, index), index, dates_dev)

        held = acc_v[...]

    send_v[...] = jnp.zeros_like(send_v)
    for owner in range(trade_n):
        send_v[owner, :, : dates_dev * factors] = held[owner * SETS_DEV : (owner + 1) * SETS_DEV]

    pl.semaphore_wait(barrier, trade_n - 1 + (date < dates_n - 1).astype(jnp.int32))

    @pl.when(date == 0)
    def _():
        state_v[...] = start
        leave(start)

    if dates_n > 2:

        @pl.when(jnp.logical_and(date > 0, date < dates_n - 1))
        def _():
            leave_copy.wait_recv()
            state = arrive_v[...].astype(jnp.float32)
            state_v[...] = state
            leave(state)

    def push(index):
        other = index + (index >= me).astype(jnp.int32)
        pltpu.make_async_remote_copy(
            src_ref=send_v.at[other],
            dst_ref=recv_v.at[me - (me > other).astype(jnp.int32)],
            send_sem=send_sem,
            recv_sem=recv_sem,
            device_id={"trade": other},
            device_id_type=MESH,
        ).start()

    each(trade_n - 1, push)

    @pl.when(date == dates_n - 1)
    def _():
        leave_copy.wait_recv()
        state_v[...] = arrive_v[...].astype(jnp.float32)

    tenor = 0.25 * (
        lax.broadcasted_iota(jnp.int32, (factors, 1), 0).astype(jnp.float32) + 1.0
    )
    discounts = []
    power = jnp.ones_like(decay)
    for step in range(dates_dev):
        power = power * decay
        now = power * state_v[...] + offset_v[step]
        discounts.append(jnp.exp(-now * tenor).astype(jnp.bfloat16))
    if width > dates_dev * factors:
        discounts.append(jnp.zeros((width - dates_dev * factors, paths), jnp.bfloat16))
    discount = jnp.concatenate(discounts, axis=0)

    everything = pltpu.make_async_copy(recv_v, recv_v, recv_sem)
    everything.wait()
    owned = send_v[me] + jnp.sum(recv_v[...], axis=0)
    lane = lax.broadcasted_iota(jnp.int32, owned.shape, 1) // factors
    owned = jnp.concatenate([jnp.where(lane == step, owned, 0.0) for step in range(dates_dev)], axis=0)
    high, low = split(owned)
    value = jnp.dot(high, discount, preferred_element_type=jnp.float32) + jnp.dot(
        low, discount, preferred_element_type=jnp.float32
    )
    mean = jnp.sum(jnp.maximum(value, 0.0), axis=1, keepdims=True) / paths
    pick = lax.broadcasted_iota(jnp.int32, (SETS_DEV, SETS_DEV), 0) == lax.broadcasted_iota(
        jnp.int32, (SETS_DEV, SETS_DEV), 1
    )
    for step in range(dates_dev):
        part = mean[step * SETS_DEV : (step + 1) * SETS_DEV]
        out_ref[step : step + 1, :] = jnp.sum(jnp.where(pick, part, 0.0), axis=0, keepdims=True)

    pltpu.make_async_copy(recv_v, recv_v, send_sem).wait()

    @pl.when(date < dates_n - 1)
    def _():
        leave_copy.wait_send()


def per_device(
    initial_term_structure,
    long_level,
    reversion,
    volatility,
    mixing,
    shocks,
    cashflows,
    maturity,
    netting,
):
    dates_dev, factors, paths = shocks.shape
    trades = cashflows.shape[1]
    dates_n = lax.axis_size("date")
    trade_n = lax.axis_size("trade")
    sets_all = SETS_DEV * trade_n
    width = -(-dates_dev * factors // LANES) * LANES
    chunks = max(1, trades // 4096)
    row = lambda x: x.reshape(1, factors)
    tall = lambda x: x.reshape(trades // LANES, LANES)
    keep = lambda x: pltpu.with_memory_space_constraint(x, pltpu.HBM)
    vmem = pl.BlockSpec(memory_space=pltpu.VMEM)
    hbm = pl.BlockSpec(memory_space=pltpu.HBM)
    return pl.pallas_call(
        functools.partial(kernel, dates_dev, dates_n, trade_n),
        out_shape=jax.ShapeDtypeStruct((dates_dev, SETS_DEV), jnp.float32),
        in_specs=[hbm] * 9,
        out_specs=vmem,
        scratch_shapes=[
            pltpu.VMEM((1, factors), jnp.float32),
            pltpu.VMEM((1, factors), jnp.float32),
            pltpu.VMEM((1, factors), jnp.float32),
            pltpu.VMEM((1, factors), jnp.float32),
            pltpu.VMEM((factors, factors), jnp.float32),
            pltpu.VMEM((trades // LANES, LANES), jnp.int32),
            pltpu.VMEM((trades // LANES, LANES), jnp.int32),
            pltpu.VMEM((dates_dev, factors, paths), jnp.float32),
            pltpu.VMEM((factors, trades), jnp.bfloat16),
            pltpu.VMEM((max(dates_dev + 1, dates_dev * dates_n), trades // LANES, LANES), jnp.float32),
            pltpu.VMEM((sets_all, dates_dev * factors), jnp.float32),
            pltpu.VMEM((dates_dev, factors, paths), jnp.float32),
            pltpu.VMEM((factors, paths), jnp.float32),
            pltpu.VMEM((factors, paths), jnp.bfloat16),
            pltpu.VMEM((factors, paths), jnp.bfloat16),
            pltpu.VMEM((trade_n, SETS_DEV, width), jnp.float32),
            pltpu.VMEM((trade_n - 1, SETS_DEV, width), jnp.float32),
            pltpu.SemaphoreType.DMA((8,)),
            pltpu.SemaphoreType.DMA((chunks,)),
            pltpu.SemaphoreType.DMA,
            pltpu.SemaphoreType.DMA,
            pltpu.SemaphoreType.DMA,
            pltpu.SemaphoreType.DMA,
        ],
        compiler_params=pltpu.CompilerParams(
            collective_id=0, has_side_effects=True, vmem_limit_bytes=24 * 1024 * 1024
        ),
    )(
        keep(row(initial_term_structure)),
        keep(row(long_level)),
        keep(row(reversion)),
        keep(row(volatility)),
        keep(mixing),
        keep(shocks),
        keep(cashflows),
        keep(tall(maturity)),
        keep(tall(netting)),
    )


def solution(mesh):
    return jax.shard_map(
        per_device,
        mesh=mesh,
        in_specs=(
            P(),
            P(),
            P(),
            P(),
            P(),
            P("date", None, None),
            P(None, "trade"),
            P("trade"),
            P("trade"),
        ),
        out_specs=P("date", "trade"),
        check_vma=False,
    )
```

```python
import functools
import math

import jax
import jax.numpy as jnp
from jax import lax
from jax.experimental import pallas as pl
from jax.experimental.pallas import tpu as pltpu
from jax.sharding import PartitionSpec as P

SETS_DEV = 4
LANES = 128
MESH = pl.DeviceIdType.MESH


def each(count, body):
    if count <= 16:
        for index in range(count):
            body(index)
    else:
        pl.loop(0, count)(body)


def split(x):
    high = x.astype(jnp.bfloat16)
    low = (x - high.astype(jnp.float32)).astype(jnp.bfloat16)
    return high, low


def kernel(
    dates_dev,
    dates_n,
    trade_n,
    start_hbm,
    level_hbm,
    speed_hbm,
    vol_hbm,
    mixing_hbm,
    shocks_hbm,
    cash_hbm,
    maturity_hbm,
    netting_hbm,
    out_ref,
    start_ref,
    level_ref,
    speed_ref,
    vol_ref,
    mixing_ref,
    maturity_ref,
    netting_ref,
    shocks_v,
    cash_v,
    code_v,
    acc_v,
    offset_v,
    state_v,
    leave_v,
    arrive_v,
    send_v,
    recv_v,
    load_sem,
    cash_sem,
    leave_sem,
    arrive_sem,
    send_sem,
    recv_sem,
):
    factors, trades = cash_v.shape
    paths = shocks_v.shape[2]
    chunks = cash_sem.shape[0]
    chunk = trades // chunks
    sets_all = SETS_DEV * trade_n
    maturities = dates_dev * dates_n
    width = send_v.shape[2]
    date = lax.axis_index("date")
    me = lax.axis_index("trade")

    loads = [
        pltpu.make_async_copy(source, target, load_sem.at[place])
        for place, (source, target) in enumerate(
            (
                (shocks_hbm, shocks_v),
                (mixing_hbm, mixing_ref),
                (start_hbm, start_ref),
                (level_hbm, level_ref),
                (speed_hbm, speed_ref),
                (vol_hbm, vol_ref),
                (maturity_hbm, maturity_ref),
                (netting_hbm, netting_ref),
            )
        )
    ]
    for load in loads:
        load.start()

    def cash_copy(index):
        part = pl.ds(pl.multiple_of(index * chunk, chunk), chunk)
        return pltpu.make_async_copy(cash_hbm.at[:, part], cash_v.at[:, part], cash_sem.at[index])

    for index in range(chunks):
        cash_copy(index).start()

    barrier = pltpu.get_barrier_semaphore()

    def greet(index):
        other = lax.rem(me + 1 + index, trade_n)
        pl.semaphore_signal(barrier, inc=1, device_id={"trade": other}, device_id_type=MESH)

    each(trade_n - 1, greet)

    @pl.when(date > 0)
    def _():
        pl.semaphore_signal(barrier, inc=1, device_id={"date": date - 1}, device_id_type=MESH)

    for load in loads[6:]:
        load.wait()

    common = math.lcm(*range(1, maturities + 1))
    whole = common <= 256
    if whole:
        expiry = maturity_ref[...]
        share = jnp.zeros_like(expiry)
        for m in range(1, maturities + 1):
            share = jnp.where(expiry == m, common // m, share)
        code_v[dates_dev] = netting_ref[...].astype(jnp.float32)
        for step in range(dates_dev):
            left = jnp.maximum(expiry - (date * dates_dev + step), 0)
            code_v[step] = (share * left).astype(jnp.float32)
    else:
        for m in range(1, maturities + 1):
            code_v[m - 1] = jnp.where(maturity_ref[...] == m, netting_ref[...], -1).astype(
                jnp.float32
            )

    tiles = sets_all // 16
    place = lax.broadcasted_iota(jnp.int32, (16, LANES), 0).astype(jnp.float32)
    marks = [(place + 16.0 * i).astype(jnp.bfloat16) for i in range(tiles)]
    one = jnp.ones((16, LANES), jnp.bfloat16)
    zero = jnp.zeros((16, LANES), jnp.bfloat16)
    rows = chunk // LANES

    def members(m, index):
        pieces = []
        for r in range(rows):
            code = jnp.broadcast_to(code_v[m, pl.ds(index * rows + r, 1), :], (16, LANES))
            code = code.astype(jnp.bfloat16)
            pieces.append(
                jnp.concatenate([jnp.where(code == mark, one, zero) for mark in marks], axis=0)
            )
        return jnp.concatenate(pieces, axis=1)

    def weighted(index):
        pieces = []
        for r in range(rows):
            spread = [
                jnp.broadcast_to(
                    code_v[step, pl.ds(index * rows + r, 1), :], (16, LANES)
                ).astype(jnp.bfloat16)
                for step in range(dates_dev + 1)
            ]
            same = [spread[-1] == mark for mark in marks]
            pieces.append(
                jnp.concatenate(
                    [jnp.where(here, share, zero) for share in spread[:-1] for here in same], axis=0
                )
            )
        return jnp.concatenate(pieces, axis=1)

    def summed(member, index, copies):
        cash = cash_v[:, pl.ds(pl.multiple_of(index * chunk, chunk), chunk)]
        cash = jnp.concatenate([cash] * copies, axis=0)
        return lax.dot_general(
            member, cash, (((1,), (1,)), ((), ())), preferred_element_type=jnp.float32
        )

    lane = lax.broadcasted_iota(jnp.int32, (1, dates_dev * factors), 1)
    at_date = date * dates_dev + lane // factors

    def weight(m):
        return jnp.maximum(m - at_date, 0).astype(jnp.float32) / jnp.full_like(
            at_date, m
        ).astype(jnp.float32)

    if whole:
        total = jnp.zeros((dates_dev * sets_all, factors), jnp.float32)
        for index in range(chunks):
            cash_copy(index).wait()
            total = total + summed(weighted(index), index, 1)
        total = total * (1.0 / common)
        held = jnp.concatenate(
            [total[step * sets_all : (step + 1) * sets_all] for step in range(dates_dev)], axis=1
        )
    else:
        acc_v[...] = jnp.zeros_like(acc_v)
        for index in range(chunks):
            cash_copy(index).wait()

        @pl.loop(0, chunks)
        def _(index):
            @pl.loop(0, maturities)
            def _(m):
                acc_v[...] += weight(m + 1) * summed(members(m, index), index, dates_dev)

        held = acc_v[...]

    if width > dates_dev * factors:
        filler = jnp.zeros((sets_all, width - dates_dev * factors), jnp.float32)
        held = jnp.concatenate([held, filler], axis=1)
    for owner in range(trade_n):
        send_v[owner] = held[owner * SETS_DEV : (owner + 1) * SETS_DEV]

    pl.semaphore_wait(barrier, trade_n - 1 + (date < dates_n - 1).astype(jnp.int32))


    def push(index):
        other = index + (index >= me).astype(jnp.int32)
        pltpu.make_async_remote_copy(
            src_ref=send_v.at[other],
            dst_ref=recv_v.at[me - (me > other).astype(jnp.int32)],
            send_sem=send_sem,
            recv_sem=recv_sem,
            device_id={"trade": other},
            device_id_type=MESH,
        ).start()

    each(trade_n - 1, push)

    for load in loads[:6]:
        load.wait()

    diagonal = lax.broadcasted_iota(jnp.int32, (factors, factors), 0) == lax.broadcasted_iota(
        jnp.int32, (factors, factors), 1
    )

    def column(ref):
        return jnp.sum(jnp.where(diagonal, ref[...], 0.0), axis=1, keepdims=True)

    decay = jnp.exp(-0.25 * column(speed_ref))
    drift = (1.0 - decay) * column(level_ref)
    start = jnp.broadcast_to(column(start_ref), (factors, paths))
    mix_high, mix_low = split(column(vol_ref) * mixing_ref[...])
    mix = jnp.concatenate([mix_high, mix_high, mix_low], axis=1)

    running = None
    power = jnp.ones_like(decay)
    for step in range(dates_dev):
        high, low = split(shocks_v[step])
        moved = jnp.dot(
            mix, jnp.concatenate([high, low, high], axis=0), preferred_element_type=jnp.float32
        )
        running = drift + moved if step == 0 else decay * running + drift + moved
        power = power * decay
        offset_v[step] = running

    leave_copy = pltpu.make_async_remote_copy(
        src_ref=leave_v,
        dst_ref=arrive_v,
        send_sem=leave_sem,
        recv_sem=arrive_sem,
        device_id={"date": date + 1},
        device_id_type=MESH,
    )

    def leave(state):
        leave_v[...] = (power * state + running).astype(jnp.bfloat16)
        leave_copy.start()

    @pl.when(date == 0)
    def _():
        state_v[...] = start
        leave(start)

    if dates_n > 2:

        @pl.when(jnp.logical_and(date > 0, date < dates_n - 1))
        def _():
            leave_copy.wait_recv()
            state = arrive_v[...].astype(jnp.float32)
            state_v[...] = state
            leave(state)


    @pl.when(date == dates_n - 1)
    def _():
        leave_copy.wait_recv()
        state_v[...] = arrive_v[...].astype(jnp.float32)

    tenor = 0.25 * (
        lax.broadcasted_iota(jnp.int32, (factors, 1), 0).astype(jnp.float32) + 1.0
    )
    discounts = []
    power = jnp.ones_like(decay)
    for step in range(dates_dev):
        power = power * decay
        now = power * state_v[...] + offset_v[step]
        discounts.append(jnp.exp(-now * tenor).astype(jnp.bfloat16))
    if width > dates_dev * factors:
        discounts.append(jnp.zeros((width - dates_dev * factors, paths), jnp.bfloat16))
    discount = jnp.concatenate(discounts, axis=0)

    everything = pltpu.make_async_copy(recv_v, recv_v, recv_sem)
    everything.wait()
    owned = send_v[me] + jnp.sum(recv_v[...], axis=0)
    lane = lax.broadcasted_iota(jnp.int32, owned.shape, 1) // factors
    owned = jnp.concatenate([jnp.where(lane == step, owned, 0.0) for step in range(dates_dev)], axis=0)
    high, low = split(owned)
    value = jnp.dot(high, discount, preferred_element_type=jnp.float32) + jnp.dot(
        low, discount, preferred_element_type=jnp.float32
    )
    mean = jnp.sum(jnp.maximum(value, 0.0), axis=1, keepdims=True) / paths
    pick = lax.broadcasted_iota(jnp.int32, (SETS_DEV, SETS_DEV), 0) == lax.broadcasted_iota(
        jnp.int32, (SETS_DEV, SETS_DEV), 1
    )
    for step in range(dates_dev):
        part = mean[step * SETS_DEV : (step + 1) * SETS_DEV]
        out_ref[step : step + 1, :] = jnp.sum(jnp.where(pick, part, 0.0), axis=0, keepdims=True)

    pltpu.make_async_copy(recv_v, recv_v, send_sem).wait()

    @pl.when(date < dates_n - 1)
    def _():
        leave_copy.wait_send()


def per_device(
    initial_term_structure,
    long_level,
    reversion,
    volatility,
    mixing,
    shocks,
    cashflows,
    maturity,
    netting,
):
    dates_dev, factors, paths = shocks.shape
    trades = cashflows.shape[1]
    dates_n = lax.axis_size("date")
    trade_n = lax.axis_size("trade")
    sets_all = SETS_DEV * trade_n
    width = -(-dates_dev * factors // LANES) * LANES
    chunks = max(1, trades // 4096)
    row = lambda x: x.reshape(1, factors)
    tall = lambda x: x.reshape(trades // LANES, LANES)
    keep = lambda x: pltpu.with_memory_space_constraint(x, pltpu.HBM)
    vmem = pl.BlockSpec(memory_space=pltpu.VMEM)
    hbm = pl.BlockSpec(memory_space=pltpu.HBM)
    return pl.pallas_call(
        functools.partial(kernel, dates_dev, dates_n, trade_n),
        out_shape=jax.ShapeDtypeStruct((dates_dev, SETS_DEV), jnp.float32),
        in_specs=[hbm] * 9,
        out_specs=vmem,
        scratch_shapes=[
            pltpu.VMEM((1, factors), jnp.float32),
            pltpu.VMEM((1, factors), jnp.float32),
            pltpu.VMEM((1, factors), jnp.float32),
            pltpu.VMEM((1, factors), jnp.float32),
            pltpu.VMEM((factors, factors), jnp.float32),
            pltpu.VMEM((trades // LANES, LANES), jnp.int32),
            pltpu.VMEM((trades // LANES, LANES), jnp.int32),
            pltpu.VMEM((dates_dev, factors, paths), jnp.float32),
            pltpu.VMEM((factors, trades), jnp.bfloat16),
            pltpu.VMEM((max(dates_dev + 1, dates_dev * dates_n), trades // LANES, LANES), jnp.float32),
            pltpu.VMEM((sets_all, dates_dev * factors), jnp.float32),
            pltpu.VMEM((dates_dev, factors, paths), jnp.float32),
            pltpu.VMEM((factors, paths), jnp.float32),
            pltpu.VMEM((factors, paths), jnp.bfloat16),
            pltpu.VMEM((factors, paths), jnp.bfloat16),
            pltpu.VMEM((trade_n, SETS_DEV, width), jnp.float32),
            pltpu.VMEM((trade_n - 1, SETS_DEV, width), jnp.float32),
            pltpu.SemaphoreType.DMA((8,)),
            pltpu.SemaphoreType.DMA((chunks,)),
            pltpu.SemaphoreType.DMA,
            pltpu.SemaphoreType.DMA,
            pltpu.SemaphoreType.DMA,
            pltpu.SemaphoreType.DMA,
        ],
        compiler_params=pltpu.CompilerParams(
            collective_id=0, has_side_effects=True, vmem_limit_bytes=24 * 1024 * 1024
        ),
    )(
        keep(row(initial_term_structure)),
        keep(row(long_level)),
        keep(row(reversion)),
        keep(row(volatility)),
        keep(mixing),
        keep(shocks),
        keep(cashflows),
        keep(tall(maturity)),
        keep(tall(netting)),
    )


def solution(mesh):
    return jax.shard_map(
        per_device,
        mesh=mesh,
        in_specs=(
            P(),
            P(),
            P(),
            P(),
            P(),
            P("date", None, None),
            P(None, "trade"),
            P("trade"),
            P("trade"),
        ),
        out_specs=P("date", "trade"),
        check_vma=False,
    )
```
